32 devices in a mesh: grp: 2 (over y), seq: 16 (over z, x, core).
Axes of the slice: x: 2, y: 2, z: 4, core: 2. Of those that a mesh axis runs over, the one named last changes fastest.
Arguments:
- values: bfloat16 [524288, 768], P(('grp', 'seq')), parts along dimension 0, may hold values from -6 to 6
- gate_in: bfloat16 [1024, 16, 768], P(('grp', 'seq')), parts along dimension 0, may hold values from -6 to 6
- cotangent: bfloat16 [1024, 16, 768], P(('grp', 'seq')), parts along dimension 0, may hold values from -1.1953125 to 1.1953125
- first_factor: bfloat16 [512, 16, 512], P('seq'), may hold values from -0.25 to 0.25
- second_factor: bfloat16 [16, 512, 512], P('seq'), may hold values from -0.25 to 0.25
Outputs:
- mixed: bfloat16 [1024, 16, 768], P(('grp', 'seq')), parts along dimension 0
- values_grad: bfloat16 [524288, 768], P(('grp', 'seq')), parts along dimension 0
- gate_grad: bfloat16 [1024, 16, 768], P(('grp', 'seq')), parts along dimension 0
- first_grad: bfloat16 [1024, 16, 512], P(('grp', 'seq')), parts along dimension 0
- second_grad: bfloat16 [32, 512, 512], P(('grp', 'seq')), parts along dimension 0
The draws below stay inside these ranges and needn't reach their ends.
There are 2 independent parts, one for each index of `grp`. The reference program is written for one: setup_inputs(seed, part) draws one part's arguments, and reference() takes and returns one part's arrays. A program takes and returns all parts, laid end to end along the dimension named above; an argument that names none is the same for every part. Nothing has to cross between parts.
All inputs are finite; a program needn't handle non-finite values.
Results may differ from the reference program's by a relative error of at most 0.0058.
Values may be sent and summed in bfloat16 or wider, within the bound.
No kernel may reach another device: no remote copies, remote signals or barrier semaphores. Data moves between devices by JAX's collectives and lax.ppermute only.
A program may use at most 128 MiB of HBM per device.

```python
import jax
import jax.numpy as jnp

C = 768
B1 = 512
B2 = 512
Q = 16
LENGTH = 262144


def shard_levels(own_key, extent, split, low, largest):
    def one(position, blocks):
        steps = jax.random.uniform(jax.random.fold_in(jax.random.fold_in(own_key, 6), position), (blocks,), jnp.float32, low / len(split), largest / len(split))
        return jnp.repeat(jnp.exp(steps), extent[position] // blocks).reshape((-1,) + (1,) * (len(extent) - position - 1))

    loudness = one(*split[0])
    for cut in split[1:]:
        loudness = loudness * one(*cut)
    return loudness


def centred(rng, extent, spread, reach, cuts=(), dtype=jnp.bfloat16):
    gain = shard_levels(rng, extent, cuts, -0.22, 0.18) if cuts else 1.0
    array = jax.random.normal(rng, extent, jnp.float32) * spread * gain
    return jnp.minimum(jnp.maximum(array, -reach), reach).astype(dtype)


def setup_inputs(seed: int = 0, part: int = 0) -> dict:
    streams_of = jax.random.split(jax.random.key(seed), 6)
    own_keys = jax.random.split(jax.random.fold_in(streams_of[5], part), 6)
    return {
        "values": centred(own_keys[0], (LENGTH, C), 1.0, 6.0, ((0, 16),)),
        "gate_in": centred(own_keys[1], (B2, Q, C), 1.0, 6.0, ((0, 16),)),
        "cotangent": centred(own_keys[2], (B2, Q, C), 0.2, 1.1953125, ((0, 16),)),
        "first_factor": centred(streams_of[3], (B2, Q, B1), B1 ** -0.5, 0.25, ((0, 16),)),
        "second_factor": centred(streams_of[4], (Q, B2, B2), B2 ** -0.5, 0.25, ((0, 16),)),
    }


def reference(values, gate_in, cotangent, first_factor, second_factor):
    wide = jnp.float32
    narrow = jnp.bfloat16
    blocks_x = values.reshape(B2, B1, C).astype(wide)
    gate_r = gate_in.astype(wide)
    cot_r = cotangent.astype(wide)
    first_w = first_factor.astype(wide)
    second_w = second_factor.astype(wide)
    inner = jnp.einsum('aqp,apc->aqc', first_w, blocks_x).astype(narrow).astype(wide)
    outer = jnp.einsum('qxa,aqc->xqc', second_w, inner).astype(narrow).astype(wide)
    mixed = (gate_r * outer).astype(narrow)
    gate_grad = (cot_r * outer).astype(narrow)
    gated = (gate_r * cot_r).astype(narrow).astype(wide)
    second_grad = jnp.einsum('xqc,aqc->qxa', gated, inner).astype(narrow)
    back_inner = jnp.einsum('qxa,xqc->aqc', second_w, gated).astype(narrow).astype(wide)
    first_grad = jnp.einsum('aqc,apc->aqp', back_inner, blocks_x).astype(narrow)
    values_grad = jnp.einsum('aqp,aqc->apc', first_w, back_inner).astype(narrow).reshape(LENGTH, C)
    return mixed, values_grad, gate_grad, first_grad, second_grad
```

```python
import functools

import jax
import jax.numpy as jnp
from jax import lax
from jax.experimental import pallas as pl
from jax.experimental.pallas import tpu as pltpu
from jax.sharding import PartitionSpec as P

WIDE = jnp.float32
NARROW = jnp.bfloat16
MIB = 1 << 20
VMEM = pltpu.VMEM
ANY = pl.ANY


def params(mib):
    return pltpu.CompilerParams(vmem_limit_bytes=mib * MIB)


def cost(flops, nbytes):
    return pl.CostEstimate(flops=flops, bytes_accessed=nbytes, transcendentals=0)


def split_matrix(rank, rows, n, order):
    total = rows * n
    shape = (total, total)
    i = lax.broadcasted_iota(jnp.int32, shape, 0)
    j = lax.broadcasted_iota(jnp.int32, shape, 1)
    slab, block = i // rows, i % rows
    k = order(slab)
    return ((j // n == block) & (j % n == (rank ^ k))).astype(NARROW)


def merge_matrix(rank, rows, n, order):
    total = rows * n
    shape = (total, total)
    i = lax.broadcasted_iota(jnp.int32, shape, 0)
    j = lax.broadcasted_iota(jnp.int32, shape, 1)
    slab, block = j // rows, j % rows
    k = order(slab)
    return ((i // n == block) & (i % n == (rank ^ k))).astype(NARROW)


def outer_major(inner):
    return lambda slab: slab


def inner_major(inner, outer):
    return lambda slab: (slab % outer) * inner + slab // outer


def dot(a, b, dims):
    return lax.dot_general(a, b, ((dims[0], dims[1]), ((), ())), preferred_element_type=WIDE)


def gated_kernel(inner, outer, rows, chunks, g_ref, d_ref, *refs):
    out_refs, matrix = refs[:outer], refs[outer]
    n = inner * outer

    @pl.when(pl.program_id(0) == 0)
    def _():
        matrix[...] = split_matrix(lax.axis_index("seq"), rows, n, outer_major(inner))

    gated = (g_ref[...].astype(WIDE) * d_ref[...].astype(WIDE)).astype(NARROW)
    span = inner * rows
    for o in range(outer):
        out_refs[o][...] = dot(matrix[o * span : (o + 1) * span, :], gated, ((1,), (0,))).astype(NARROW)


def gated_slabs(gate_in, cotangent, inner, outer):
    rows, n, channels = gate_in.shape
    total = rows * n
    chunks = 3 if channels % 384 == 0 else 1
    wide = channels // chunks
    span = inner * rows
    out = pl.pallas_call(
        functools.partial(gated_kernel, inner, outer, rows, chunks),
        grid=(chunks,),
        in_specs=[pl.BlockSpec((total, wide), lambda i: (0, i))] * 2,
        out_specs=[pl.BlockSpec((span, wide), lambda i: (0, i))] * outer,
        out_shape=[jax.ShapeDtypeStruct((span, channels), NARROW)] * outer,
        scratch_shapes=[VMEM((total, total), NARROW)],
        compiler_params=params(32),
        cost_estimate=cost(2 * total * total * channels, 6 * total * channels),
        name="gated_slabs",
    )(gate_in.reshape(total, channels), cotangent.reshape(total, channels))
    return [o.reshape(inner, rows, channels) for o in out]


def inner_kernel(inner, outer, slots, group, w_ref, x_ref, *refs):
    out_refs, (kept, buf, sem) = refs[:inner], refs[inner:]
    blocks, n, length = w_ref.shape
    steps = blocks // group
    rows = group * length

    def fetch(i, s):
        return pltpu.make_async_copy(x_ref.at[pl.ds(i * rows, rows), :], buf.at[s], sem.at[s])

    for s in range(slots):
        fetch(s, s).start()
    matrix = split_matrix(lax.axis_index("seq"), blocks, n, inner_major(inner, outer))

    def step(i, carry):
        s = lax.rem(i, slots)
        fetch(i, s).wait()
        for g in range(group):
            u = dot(w_ref[i * group + g], buf[s, g * length : (g + 1) * length, :], ((1,), (0,)))
            kept[pl.ds(pl.multiple_of((i * group + g) * n, n), n), :] = u.astype(NARROW)

        @pl.when(i + slots < steps)
        def _():
            fetch(i + slots, s).start()

        return carry

    lax.fori_loop(0, steps, step, 0)
    span = outer * blocks
    for o in range(inner):
        out_refs[o][...] = dot(matrix[o * span : (o + 1) * span, :], kept[...], ((1,), (0,))).astype(NARROW)


def inner_slabs(first_factor, values, inner, outer):
    blocks, n, length = first_factor.shape
    channels = values.shape[1]
    group = 2 if blocks % 2 == 0 else 1
    slots = min(4, blocks // group)
    span = outer * blocks
    out = pl.pallas_call(
        functools.partial(inner_kernel, inner, outer, slots, group),
        in_specs=[pl.BlockSpec(memory_space=VMEM), pl.BlockSpec(memory_space=ANY)],
        out_specs=[pl.BlockSpec(memory_space=VMEM)] * inner,
        out_shape=[jax.ShapeDtypeStruct((span, channels), NARROW)] * inner,
        scratch_shapes=[
            VMEM((blocks * n, channels), NARROW),
            VMEM((slots, group * length, channels), NARROW),
            pltpu.SemaphoreType.DMA((slots,)),
        ],
        compiler_params=params(32),
        cost_estimate=cost(2 * blocks * n * length * channels, 2 * blocks * length * channels),
        name="inner_slabs",
    )(first_factor, values)
    return [o.reshape(outer, blocks, channels) for o in out]


def mix_kernel(inner, outer, rows, arrive_inner, leave_inner, transpose, parts, s_ref, *refs):
    arrive_n = inner if arrive_inner else outer
    leave_n = inner if leave_inner else outer
    in_refs, out_refs = refs[:arrive_n], refs[arrive_n : arrive_n + leave_n * parts]
    whole_ref, product = refs[arrive_n + leave_n * parts :]
    rank = lax.axis_index("seq")

    def number(group, member, by_inner):
        return member * inner + group if by_inner else group * inner + member

    def place(k):
        return pl.ds(pl.multiple_of((rank ^ k) * rows, rows), rows)

    for a in range(arrive_n):
        for b in range(inner * outer // arrive_n):
            whole_ref[place(number(a, b, arrive_inner)), :] = in_refs[a][b]
    product[...] = dot(s_ref[0], whole_ref[...], ((0 if transpose else 1,), (0,))).astype(NARROW)
    part = rows // parts
    for a in range(leave_n):
        for b in range(inner * outer // leave_n):
            block = product[place(number(a, b, leave_inner)), :]
            for p in range(parts):
                out_refs[p * leave_n + a][b] = block[p * part : (p + 1) * part]


def mix(second_factor, slabs, inner, outer, arrive_inner, leave_inner, transpose, parts, name):
    n = inner * outer
    rows, channels = slabs[0].shape[1:]
    total = n * rows
    leave_n = inner if leave_inner else outer
    member = n // leave_n
    part = rows // parts
    out = pl.pallas_call(
        functools.partial(mix_kernel, inner, outer, rows, arrive_inner, leave_inner, transpose, parts),
        in_specs=[pl.BlockSpec(memory_space=VMEM)] * (1 + len(slabs)),
        out_specs=[pl.BlockSpec(memory_space=VMEM)] * (leave_n * parts + 1),
        out_shape=[jax.ShapeDtypeStruct((member, part, channels), NARROW)] * (leave_n * parts)
        + [jax.ShapeDtypeStruct((total, channels), NARROW)],
        scratch_shapes=[VMEM((total, channels), NARROW)],
        compiler_params=params(32),
        cost_estimate=cost(2 * total * total * channels, 4 * total * channels),
        name=name,
    )(second_factor, *slabs)
    return [out[p * leave_n : (p + 1) * leave_n] for p in range(parts)], out[-1]


def grads_kernel(inner, outer, slots, group, first, w_ref, x_ref, *refs):
    slab_refs = refs[:inner]
    refs = refs[inner:] if first else refs[inner + 2 :]
    vg_ref, fg_ref, slabs, back, fg_buf, buf, out_buf, in_sem, out_sem, fg_sem = refs
    blocks, n, length = w_ref.shape
    part = slab_refs[0].shape[1]
    base = 0 if first else blocks - part
    steps = part // group
    rows = group * length
    channels = slabs.shape[1]

    def fetch(i, s):
        return pltpu.make_async_copy(x_ref.at[pl.ds((base + i * group) * length, rows), :], buf.at[s], in_sem.at[s])

    def put(i, s):
        return pltpu.make_async_copy(out_buf.at[s], vg_ref.at[pl.ds((base + i * group) * length, rows), :], out_sem.at[s])

    for s in range(slots):
        fetch(s, s).start()
    span = outer * part
    for o in range(inner):
        for b in range(outer):
            slabs[(o * outer + b) * part : (o * outer + b + 1) * part, :] = slab_refs[o][b]
    matrix = merge_matrix(lax.axis_index("seq"), part, n, inner_major(inner, outer))
    back[...] = dot(matrix, slabs[...], ((1,), (0,))).astype(NARROW)

    def step(i, carry):
        s = lax.rem(i, slots)

        @pl.when(i >= slots)
        def _():
            put(i - slots, s).wait()

        fetch(i, s).wait()
        for g in range(group):
            w = w_ref[base + i * group + g]
            f = back[pl.ds(pl.multiple_of((i * group + g) * n, n), n), :]
            here = slice(g * length, (g + 1) * length)
            out_buf[s, here, :] = dot(w, f, ((0,), (0,))).astype(NARROW)
            fg_buf[i * group + g] = dot(f, buf[s, here, :], ((1,), (1,))).astype(NARROW)
        put(i, s).start()

        @pl.when(i + slots < steps)
        def _():
            fetch(i + slots, s).start()

        return carry

    lax.fori_loop(0, steps, step, 0)
    last = pltpu.make_async_copy(fg_buf, fg_ref.at[pl.ds(base, part)], fg_sem)
    last.start()
    for i in range(steps - slots, steps):
        put(i, i % slots).wait()
    last.wait()


def grads(first_factor, values, slabs, inner, outer, earlier):
    blocks, n, length = first_factor.shape
    channels = values.shape[1]
    part = slabs[0].shape[1]
    first = earlier is None
    group = 2 if part % 2 == 0 else 1
    slots = min(4, part // group)
    shapes = [
        jax.ShapeDtypeStruct(values.shape, NARROW),
        jax.ShapeDtypeStruct(first_factor.shape, NARROW),
    ]
    return pl.pallas_call(
        functools.partial(grads_kernel, inner, outer, slots, group, first),
        in_specs=[pl.BlockSpec(memory_space=VMEM), pl.BlockSpec(memory_space=ANY)]
        + [pl.BlockSpec(memory_space=VMEM)] * inner
        + ([] if first else [pl.BlockSpec(memory_space=ANY)] * 2),
        out_specs=[pl.BlockSpec(memory_space=ANY)] * 2,
        out_shape=shapes,
        input_output_aliases={} if first else {2 + inner: 0, 3 + inner: 1},
        scratch_shapes=[
            VMEM((part * n, channels), NARROW),
            VMEM((part * n, channels), NARROW),
            VMEM((part, n, length), NARROW),
            VMEM((slots, group * length, channels), NARROW),
            VMEM((slots, group * length, channels), NARROW),
            pltpu.SemaphoreType.DMA((slots,)),
            pltpu.SemaphoreType.DMA((slots,)),
            pltpu.SemaphoreType.DMA,
        ],
        compiler_params=params(40),
        cost_estimate=cost(4 * part * n * length * channels, 4 * part * length * channels),
        name="grads",
    )(first_factor, values, *slabs, *(() if first else earlier))


def gates_kernel(inner, outer, rows, g_ref, d_ref, *refs):
    slab_refs, (mixed_ref, grad_ref, matrix, slabs) = refs[:outer], refs[outer:]
    n = inner * outer

    @pl.when(pl.program_id(0) == 0)
    def _():
        matrix[...] = merge_matrix(lax.axis_index("seq"), rows, n, outer_major(inner))

    span = inner * rows
    for o in range(outer):
        slabs[o * span : (o + 1) * span, :] = slab_refs[o][...]
    z = dot(matrix[...], slabs[...], ((1,), (0,)))
    mixed_ref[...] = (g_ref[...].astype(WIDE) * z).astype(NARROW)
    grad_ref[...] = (d_ref[...].astype(WIDE) * z).astype(NARROW)


def gates(gate_in, cotangent, slabs, inner, outer):
    rows, n, channels = gate_in.shape
    total = rows * n
    chunks = 3 if channels % 384 == 0 else 1
    wide = channels // chunks
    span = inner * rows
    out = pl.pallas_call(
        functools.partial(gates_kernel, inner, outer, rows),
        grid=(chunks,),
        in_specs=[pl.BlockSpec((total, wide), lambda i: (0, i))] * 2
        + [pl.BlockSpec((span, wide), lambda i: (0, i))] * outer,
        out_specs=[pl.BlockSpec((total, wide), lambda i: (0, i))] * 2,
        out_shape=[jax.ShapeDtypeStruct((total, channels), NARROW)] * 2,
        scratch_shapes=[VMEM((total, total), NARROW), VMEM((total, wide), NARROW)],
        compiler_params=params(32),
        cost_estimate=cost(2 * total * total * channels, 10 * total * channels),
        name="gates",
    )(
        gate_in.reshape(total, channels),
        cotangent.reshape(total, channels),
        *[s.reshape(span, channels) for s in slabs],
    )
    return [o.reshape(gate_in.shape) for o in out]


def after(arrays, *tokens):
    return list(lax.optimization_barrier(tuple(arrays) + tokens)[: len(arrays)])


def exchange(slabs, step, n, order):
    got = list(slabs)
    for k in order:
        got[k] = lax.ppermute(slabs[k], "seq", [(i, i ^ (k * step)) for i in range(n)])
    return got


def regroup(slabs):
    count = slabs[0].shape[0]
    return [jnp.stack([s[b] for s in slabs]) for b in range(count)]


def by_permutes(values, gate_in, cotangent, first_factor, second_factor, inner, outer):
    n = inner * outer
    far = [2, 3, 1] if outer == 4 else list(range(outer - 1, 0, -1))
    near = [2, 3, 1] if inner == 4 else list(range(inner - 1, 0, -1))

    def across(slabs):
        return exchange(slabs, inner, n, far)

    def beside(slabs):
        return exchange(slabs, 1, n, near)

    e = across(gated_slabs(gate_in, cotangent, inner, outer))
    e = beside(regroup(e))
    u = beside(inner_slabs(first_factor, values, inner, outer))
    u = across(regroup(u))
    halves = 2 if gate_in.shape[0] % 32 == 0 else 1
    f, e_all = mix(second_factor, e, inner, outer, True, False, True, halves, "back")
    z, u_all = mix(second_factor, u, inner, outer, False, True, False, 1, "forth")
    z = across(regroup(beside(z[0])))
    out = None
    for half in f:
        out = grads(first_factor, values, beside(regroup(across(half))), inner, outer, out)
    values_grad, first_grad = out
    second_grad = dot(e_all, u_all, ((1,), (1,))).astype(NARROW)[None]
    mixed, gate_grad = gates(gate_in, cotangent, z, inner, outer)
    return mixed, values_grad, gate_grad, first_grad, second_grad


def by_all_to_all(values, gate_in, cotangent, first_factor, second_factor):
    block_len = first_factor.shape[2]
    channels = values.shape[1]
    blocks_x = values.reshape(-1, block_len, channels)
    inner = jnp.einsum("aqp,apc->aqc", first_factor, blocks_x, preferred_element_type=WIDE).astype(NARROW)
    gated = (gate_in.astype(WIDE) * cotangent.astype(WIDE)).astype(NARROW)
    inner_t = lax.all_to_all(inner, "seq", split_axis=1, concat_axis=0, tiled=True)
    outer_t = jnp.einsum("qxa,aqc->xqc", second_factor, inner_t, preferred_element_type=WIDE).astype(NARROW)
    outer = lax.all_to_all(outer_t, "seq", split_axis=0, concat_axis=1, tiled=True)
    gated_t = lax.all_to_all(gated, "seq", split_axis=1, concat_axis=0, tiled=True)
    second_grad = jnp.einsum("xqc,aqc->qxa", gated_t, inner_t, preferred_element_type=WIDE).astype(NARROW)
    back_t = jnp.einsum("qxa,xqc->aqc", second_factor, gated_t, preferred_element_type=WIDE).astype(NARROW)
    back_inner = lax.all_to_all(back_t, "seq", split_axis=0, concat_axis=1, tiled=True)
    outer_f = outer.astype(WIDE)
    mixed = (gate_in.astype(WIDE) * outer_f).astype(NARROW)
    gate_grad = (cotangent.astype(WIDE) * outer_f).astype(NARROW)
    first_grad = jnp.einsum("aqc,apc->aqp", back_inner, blocks_x, preferred_element_type=WIDE).astype(NARROW)
    values_grad = (
        jnp.einsum("aqp,aqc->apc", first_factor, back_inner, preferred_element_type=WIDE)
        .astype(NARROW)
        .reshape(-1, channels)
    )
    return mixed, values_grad, gate_grad, first_grad, second_grad


def solution(mesh):
    n = mesh.shape["seq"]

    def on_device(values, gate_in, cotangent, first_factor, second_factor):
        rows, kept = gate_in.shape[:2]
        if n == 16 and kept == n and rows % 16 == 0 and first_factor.shape[0] == rows:
            return by_permutes(values, gate_in, cotangent, first_factor, second_factor, 4, n // 4)
        return by_all_to_all(values, gate_in, cotangent, first_factor, second_factor)

    both = ("grp", "seq")
    return jax.shard_map(
        on_device,
        mesh=mesh,
        in_specs=(
            P(both, None),
            P(both, None, None),
            P(both, None, None),
            P("seq", None, None),
            P("seq", None, None),
        ),
        out_specs=(
            P(both, None, None),
            P(both, None),
            P(both, None, None),
            P(both, None, None),
            P(both, None, None),
        ),
        check_vma=False,
    )
```

```python
import functools

import jax
import jax.numpy as jnp
from jax import lax
from jax.experimental import pallas as pl
from jax.experimental.pallas import tpu as pltpu
from jax.sharding import PartitionSpec as P

WIDE = jnp.float32
NARROW = jnp.bfloat16
MIB = 1 << 20
VMEM = pltpu.VMEM
ANY = pltpu.HBM


def params(mib):
    return pltpu.CompilerParams(vmem_limit_bytes=mib * MIB)


def cost(flops, nbytes):
    return pl.CostEstimate(flops=flops, bytes_accessed=nbytes, transcendentals=0)


def split_matrix(rank, rows, n, order):
    total = rows * n
    shape = (total, total)
    i = lax.broadcasted_iota(jnp.int32, shape, 0)
    j = lax.broadcasted_iota(jnp.int32, shape, 1)
    slab, block = i // rows, i % rows
    k = order(slab)
    return ((j // n == block) & (j % n == (rank ^ k))).astype(NARROW)


def merge_matrix(rank, rows, n, order):
    total = rows * n
    shape = (total, total)
    i = lax.broadcasted_iota(jnp.int32, shape, 0)
    j = lax.broadcasted_iota(jnp.int32, shape, 1)
    slab, block = j // rows, j % rows
    k = order(slab)
    return ((i // n == block) & (i % n == (rank ^ k))).astype(NARROW)


def count_of(n, mode):
    by_inner, inner = mode
    return inner if by_inner else n // inner


def number(mode, group, member):
    by_inner, inner = mode
    return member * inner + group if by_inner else group * inner + member


def major(n, mode):
    each = n // count_of(n, mode)
    return lambda place: number(mode, place // each, place % each)


def dot(a, b, dims):
    return lax.dot_general(a, b, (dims, ((), ())), preferred_element_type=WIDE)


def gated_kernel(n, mode, rows, g_ref, d_ref, *refs):
    count = count_of(n, mode)
    out_refs, matrix = refs[:count], refs[count]
    @pl.when(pl.program_id(0) == 0)
    def _():
        matrix[...] = split_matrix(lax.axis_index("seq"), rows, n, major(n, mode))

    gated = (g_ref[...].astype(WIDE) * d_ref[...].astype(WIDE)).astype(NARROW)
    span = n // count * rows
    for o in range(count):
        out_refs[o][...] = dot(matrix[o * span : (o + 1) * span, :], gated, ((1,), (0,))).astype(NARROW)


def gated_slabs(gate_in, cotangent, mode):
    rows, n, channels = gate_in.shape
    total = rows * n
    chunks = 3 if channels % 384 == 0 else 1
    wide = channels // chunks
    count = count_of(n, mode)
    span = n // count * rows
    out = pl.pallas_call(
        functools.partial(gated_kernel, n, mode, rows),
        grid=(chunks,),
        in_specs=[pl.BlockSpec((total, wide), lambda i: (0, i))] * 2,
        out_specs=[pl.BlockSpec((span, wide), lambda i: (0, i))] * count,
        out_shape=[jax.ShapeDtypeStruct((span, channels), NARROW)] * count,
        scratch_shapes=[VMEM((total, total), NARROW)],
        compiler_params=params(58),
        cost_estimate=cost(2 * total * total * channels, 6 * total * channels),
        name="gated_slabs",
    )(gate_in.reshape(total, channels), cotangent.reshape(total, channels))
    return [o.reshape(n // count, rows, channels) for o in out]


def inner_kernel(mode, group, w_ref, x_ref, *refs):
    n, length = w_ref.shape[1:]
    count = count_of(n, mode)
    out_refs, (kept_a, kept_b, kept, sem) = refs[:count], refs[count:]
    rows = group * length
    blocks = w_ref.shape[0]
    steps = blocks // group // 2

    def fetch(i, kept_x, base):
        here = pl.ds(pl.multiple_of(i * rows, rows), rows)
        there = pl.ds(pl.multiple_of((base + i) * rows, rows), rows)
        return pltpu.make_async_copy(x_ref.at[there, :], kept_x.at[here, :], sem.at[base + i])

    parts = ((kept_a, 0), (kept_b, steps))
    for kept_x, base in parts:
        for i in range(steps):
            fetch(i, kept_x, base).start()
    matrix = split_matrix(lax.axis_index("seq"), blocks, n, major(n, mode))
    for kept_x, base in parts:

        def step(i, carry, kept_x=kept_x, base=base):
            fetch(i, kept_x, base).wait()
            for g in range(group):
                block = (base + i) * group + g
                x = kept_x[pl.ds(pl.multiple_of((i * group + g) * length, length), length), :]
                u = dot(w_ref[block], x, ((1,), (0,)))
                kept[pl.ds(pl.multiple_of(block * n, n), n), :] = u.astype(NARROW)
            return carry

        lax.fori_loop(0, steps, step, 0)
    span = n // count * blocks
    for o in range(count):
        out_refs[o][...] = dot(matrix[o * span : (o + 1) * span, :], kept[...], ((1,), (0,))).astype(NARROW)


def inner_slabs(first_factor, values, mode):
    blocks, n, length = first_factor.shape
    channels = values.shape[1]
    group = 2 if blocks % 4 == 0 else 1
    count = count_of(n, mode)
    span = n // count * blocks
    half = VMEM((blocks // 2 * length, channels), NARROW)
    *out, kept_a, kept_b = pl.pallas_call(
        functools.partial(inner_kernel, mode, group),
        in_specs=[pl.BlockSpec(memory_space=VMEM), pl.BlockSpec(memory_space=ANY)],
        out_specs=[pl.BlockSpec(memory_space=VMEM)] * (count + 2),
        out_shape=[jax.ShapeDtypeStruct((span, channels), NARROW)] * count + [half] * 2,
        scratch_shapes=[VMEM((blocks * n, channels), NARROW), pltpu.SemaphoreType.DMA((blocks // group,))],
        compiler_params=params(32),
        cost_estimate=cost(2 * blocks * n * length * channels, 2 * blocks * length * channels),
        name="inner_slabs",
    )(first_factor, values)
    return [o.reshape(n // count, blocks, channels) for o in out], [kept_a, kept_b]


def mix_kernel(n, arrive, leave, transpose, s_ref, *refs):
    (arrive_mode, arrive_parts), (leave_mode, leave_parts) = arrive, leave
    arrive_n = count_of(n, arrive_mode)
    leave_n = count_of(n, leave_mode)
    in_refs = refs[: arrive_n * arrive_parts]
    out_refs = refs[arrive_n * arrive_parts :][: leave_n * leave_parts]
    whole_ref, product = refs[arrive_n * arrive_parts + leave_n * leave_parts :]
    rank = lax.axis_index("seq")
    rows = whole_ref.shape[0] // n

    def place(group, member, mode, part, parts):
        k = number(mode, group, member)
        size = rows // parts
        return pl.ds(pl.multiple_of((rank ^ k) * rows + part * size, size), size)

    for p in range(arrive_parts):
        for a in range(arrive_n):
            for b in range(n // arrive_n):
                whole_ref[place(a, b, arrive_mode, p, arrive_parts), :] = in_refs[p * arrive_n + a][b]
    product[...] = dot(s_ref[0], whole_ref[...], ((0 if transpose else 1,), (0,))).astype(NARROW)
    for p in range(leave_parts):
        for a in range(leave_n):
            for b in range(n // leave_n):
                out_refs[p * leave_n + a][b] = product[place(a, b, leave_mode, p, leave_parts), :]


def mix(second_factor, slabs, n, arrive, leave, transpose, name):
    total = second_factor.shape[1]
    channels = slabs[0][0].shape[2]
    leave_n = count_of(n, leave[0])
    part = total // n // leave[1]
    flat = [s for half in slabs for s in half]
    out = pl.pallas_call(
        functools.partial(mix_kernel, n, arrive, leave, transpose),
        in_specs=[pl.BlockSpec(memory_space=VMEM)] * (1 + len(flat)),
        out_specs=[pl.BlockSpec(memory_space=VMEM)] * (leave_n * leave[1] + 1),
        out_shape=[jax.ShapeDtypeStruct((n // leave_n, part, channels), NARROW)] * (leave_n * leave[1])
        + [jax.ShapeDtypeStruct((total, channels), NARROW)],
        scratch_shapes=[VMEM((total, channels), NARROW)],
        compiler_params=params(10),
        cost_estimate=cost(2 * total * total * channels, 4 * total * channels),
        name=name,
    )(second_factor, *flat)
    return [out[p * leave_n : (p + 1) * leave_n] for p in range(leave[1])], out[-1]


def grads_kernel(mode, slots, group, half, held, w_ref, *refs):
    n, length = w_ref.shape[1:]
    x_refs, refs = refs[:held], refs[held:]
    count = count_of(n, mode)
    slab_refs = refs[:count]
    refs = refs[count:] if half == 0 else refs[count + 2 :]
    vg_ref, fg_ref, slabs, back, fg_buf, out_buf, out_sem, fg_sem = refs
    part = slab_refs[0].shape[1]
    base = half * part
    steps = part // group
    rows = group * length

    def put(i, s):
        there = pl.ds(pl.multiple_of(base * length + i * rows, rows), rows)
        return pltpu.make_async_copy(out_buf.at[s], vg_ref.at[there, :], out_sem.at[s])

    every = n // count
    for o in range(count):
        for b in range(every):
            slabs[(o * every + b) * part : (o * every + b + 1) * part, :] = slab_refs[o][b]
    matrix = merge_matrix(lax.axis_index("seq"), part, n, major(n, mode))
    back[...] = dot(matrix, slabs[...], ((1,), (0,))).astype(NARROW)

    each = steps // held

    def step(x_ref, start, i, carry):
        s = lax.rem(i, slots)

        @pl.when(i >= slots)
        def _():
            put(i - slots, s).wait()

        for g in range(group):
            block = i * group + g
            w = w_ref[base + block]
            f = back[pl.ds(pl.multiple_of(block * n, n), n), :]
            out_buf[s, g * length : (g + 1) * length, :] = dot(w, f, ((0,), (0,))).astype(NARROW)
            x = x_ref[pl.ds(pl.multiple_of((block - start * group) * length, length), length), :]
            fg_buf[block] = dot(f, x, ((1,), (1,))).astype(NARROW)
        put(i, s).start()
        return carry

    for h in range(held):
        lax.fori_loop(h * each, (h + 1) * each, functools.partial(step, x_refs[h], h * each), 0)
    last = pltpu.make_async_copy(fg_buf, fg_ref.at[pl.ds(base, part)], fg_sem)
    last.start()
    for i in range(steps - slots, steps):
        put(i, i % slots).wait()
    last.wait()


def grads(first_factor, kept_x, slabs, mode, half, earlier):
    blocks, n, length = first_factor.shape
    channels = kept_x[0].shape[1]
    held, count = len(kept_x), len(slabs)
    part = slabs[0].shape[1]
    group = next(g for g in (4, 2, 1) if part % g == 0)
    slots = min(3, part // group)
    shapes = [
        jax.ShapeDtypeStruct((blocks * length, channels), NARROW),
        jax.ShapeDtypeStruct(first_factor.shape, NARROW),
    ]
    return pl.pallas_call(
        functools.partial(grads_kernel, mode, slots, group, half, held),
        in_specs=[pl.BlockSpec(memory_space=VMEM)] * (1 + held + count)
        + ([] if half == 0 else [pl.BlockSpec(memory_space=ANY)] * 2),
        out_specs=[pl.BlockSpec(memory_space=ANY)] * 2,
        out_shape=shapes,
        input_output_aliases={} if half == 0 else {1 + held + count: 0, 2 + held + count: 1},
        scratch_shapes=[
            VMEM((part * n, channels), NARROW),
            VMEM((part * n, channels), NARROW),
            VMEM((part, n, length), NARROW),
            VMEM((slots, group * length, channels), NARROW),
            pltpu.SemaphoreType.DMA((slots,)),
            pltpu.SemaphoreType.DMA,
        ],
        compiler_params=params(16),
        cost_estimate=cost(4 * part * n * length * channels, 2 * part * length * channels),
        name="grads",
    )(first_factor, *kept_x, *slabs, *(earlier or ()))


def gates_kernel(n, mode, rows, g_ref, d_ref, *refs):
    count = count_of(n, mode)
    slab_refs, (mixed_ref, grad_ref, matrix, slabs) = refs[:count], refs[count:]
    @pl.when(pl.program_id(0) == 0)
    def _():
        matrix[...] = merge_matrix(lax.axis_index("seq"), rows, n, major(n, mode))

    span = n // count * rows
    for o in range(count):
        slabs[o * span : (o + 1) * span, :] = slab_refs[o][...]
    z = dot(matrix[...], slabs[...], ((1,), (0,)))
    mixed_ref[...] = (g_ref[...].astype(WIDE) * z).astype(NARROW)
    grad_ref[...] = (d_ref[...].astype(WIDE) * z).astype(NARROW)


def gates(gate_in, cotangent, slabs, mode):
    rows, n, channels = gate_in.shape
    total = rows * n
    chunks = 3 if channels % 384 == 0 else 1
    wide = channels // chunks
    count = count_of(n, mode)
    span = n // count * rows
    out = pl.pallas_call(
        functools.partial(gates_kernel, n, mode, rows),
        grid=(chunks,),
        in_specs=[pl.BlockSpec((total, wide), lambda i: (0, i))] * 2
        + [pl.BlockSpec((span, wide), lambda i: (0, i))] * count,
        out_specs=[pl.BlockSpec((total, wide), lambda i: (0, i))] * 2,
        out_shape=[jax.ShapeDtypeStruct((total, channels), NARROW)] * 2,
        scratch_shapes=[VMEM((total, total), NARROW), VMEM((total, wide), NARROW)],
        compiler_params=params(10),
        cost_estimate=cost(2 * total * total * channels, 10 * total * channels),
        name="gates",
    )(
        gate_in.reshape(total, channels),
        cotangent.reshape(total, channels),
        *[s.reshape(span, channels) for s in slabs],
    )
    return [o.reshape(gate_in.shape) for o in out]


def after(arrays, *tokens):
    return list(lax.optimization_barrier(tuple(arrays) + tokens)[: len(arrays)])


def regroup(slabs):
    count = slabs[0].shape[0]
    return [jnp.stack([s[b] for s in slabs]) for b in range(count)]


def by_permutes(values, gate_in, cotangent, first_factor, second_factor, inner):
    n = gate_in.shape[1]
    near, far = (True, inner), (False, inner)

    def permutes(slabs, step):
        got = list(slabs)
        count = len(slabs)
        for k in [2, 3, 1] if count == 4 else range(count - 1, 0, -1):
            got[k] = lax.ppermute(slabs[k], "seq", [(i, i ^ (k * step)) for i in range(n)])
        return got

    def across(slabs):
        return permutes(slabs, inner)

    def beside(slabs):
        return permutes(slabs, 1)

    gated = gated_slabs(gate_in, cotangent, far)
    e = across(gated)
    (factor,) = after([first_factor], gated[0])
    u, kept_x = inner_slabs(factor, values, far)
    e = beside(regroup(after(e, u[0])))
    u = across(u)
    (f,), e_all = mix(second_factor, [e], n, (near, 1), (far, 1), True, "back")
    f = across(f)
    u = beside(regroup(u))
    (z,), u_all = mix(second_factor, [u], n, (near, 1), (near, 1), False, "forth")
    z = across(regroup(beside(z)))
    f = beside(regroup(f))
    out = None
    part = gate_in.shape[0] // 2
    for half in range(2):
        slabs = [x[:, half * part : (half + 1) * part] for x in f]
        out = grads(first_factor, [kept_x[half]], slabs, near, half, out)
    values_grad, first_grad = out
    second_grad = dot(*after([e_all, u_all], first_grad), ((1,), (1,))).astype(NARROW)[None]
    gate_in, cotangent = after([gate_in, cotangent], first_grad)
    mixed, gate_grad = gates(gate_in, cotangent, z, far)
    return mixed, values_grad, gate_grad, first_grad, second_grad


def by_all_to_all(values, gate_in, cotangent, first_factor, second_factor):
    block_len = first_factor.shape[2]
    channels = values.shape[1]
    blocks_x = values.reshape(-1, block_len, channels)
    inner = jnp.einsum("aqp,apc->aqc", first_factor, blocks_x, preferred_element_type=WIDE).astype(NARROW)
    gated = (gate_in.astype(WIDE) * cotangent.astype(WIDE)).astype(NARROW)
    inner_t = lax.all_to_all(inner, "seq", split_axis=1, concat_axis=0, tiled=True)
    outer_t = jnp.einsum("qxa,aqc->xqc", second_factor, inner_t, preferred_element_type=WIDE).astype(NARROW)
    outer = lax.all_to_all(outer_t, "seq", split_axis=0, concat_axis=1, tiled=True)
    gated_t = lax.all_to_all(gated, "seq", split_axis=1, concat_axis=0, tiled=True)
    second_grad = jnp.einsum("xqc,aqc->qxa", gated_t, inner_t, preferred_element_type=WIDE).astype(NARROW)
    back_t = jnp.einsum("qxa,xqc->aqc", second_factor, gated_t, preferred_element_type=WIDE).astype(NARROW)
    back_inner = lax.all_to_all(back_t, "seq", split_axis=0, concat_axis=1, tiled=True)
    outer_f = outer.astype(WIDE)
    mixed = (gate_in.astype(WIDE) * outer_f).astype(NARROW)
    gate_grad = (cotangent.astype(WIDE) * outer_f).astype(NARROW)
    first_grad = jnp.einsum("aqc,apc->aqp", back_inner, blocks_x, preferred_element_type=WIDE).astype(NARROW)
    values_grad = (
        jnp.einsum("aqp,aqc->apc", first_factor, back_inner, preferred_element_type=WIDE)
        .astype(NARROW)
        .reshape(-1, channels)
    )
    return mixed, values_grad, gate_grad, first_grad, second_grad


def solution(mesh):
    n = mesh.shape["seq"]

    def on_device(values, gate_in, cotangent, first_factor, second_factor):
        rows, kept = gate_in.shape[:2]
        if n == 16 and kept == n and rows % 32 == 0 and first_factor.shape[0] == rows:
            return by_permutes(values, gate_in, cotangent, first_factor, second_factor, 4)
        return by_all_to_all(values, gate_in, cotangent, first_factor, second_factor)

    both = ("grp", "seq")
    return jax.shard_map(
        on_device,
        mesh=mesh,
        in_specs=(
            P(both, None),
            P(both, None, None),
            P(both, None, None),
            P("seq", None, None),
            P("seq", None, None),
        ),
        out_specs=(
            P(both, None, None),
            P(both, None),
            P(both, None, None),
            P(both, None, None),
            P(both, None, None),
        ),
        check_vma=False,
    )
```

```python
import functools

import jax
import jax.numpy as jnp
from jax import lax
from jax.experimental import pallas as pl
from jax.experimental.pallas import tpu as pltpu
from jax.sharding import PartitionSpec as P

WIDE = jnp.float32
NARROW = jnp.bfloat16
MIB = 1 << 20
VMEM = pltpu.VMEM
ANY = pltpu.HBM


def params(mib):
    return pltpu.CompilerParams(vmem_limit_bytes=mib * MIB)


def cost(flops, nbytes):
    return pl.CostEstimate(flops=flops, bytes_accessed=nbytes, transcendentals=0)


def split_matrix(rank, rows, n, order):
    total = rows * n
    shape = (total, total)
    i = lax.broadcasted_iota(jnp.int32, shape, 0)
    j = lax.broadcasted_iota(jnp.int32, shape, 1)
    slab, block = i // rows, i % rows
    k = order(slab)
    return ((j // n == block) & (j % n == (rank ^ k))).astype(NARROW)


def merge_matrix(rank, rows, n, order):
    total = rows * n
    shape = (total, total)
    i = lax.broadcasted_iota(jnp.int32, shape, 0)
    j = lax.broadcasted_iota(jnp.int32, shape, 1)
    slab, block = j // rows, j % rows
    k = order(slab)
    return ((i // n == block) & (i % n == (rank ^ k))).astype(NARROW)


def count_of(n, mode):
    by_inner, inner = mode
    return inner if by_inner else n // inner


def number(mode, group, member):
    by_inner, inner = mode
    return member * inner + group if by_inner else group * inner + member


def major(n, mode):
    each = n // count_of(n, mode)
    return lambda place: number(mode, place // each, place % each)


def dot(a, b, dims):
    return lax.dot_general(a, b, (dims, ((), ())), preferred_element_type=WIDE)


def gated_kernel(n, mode, rows, g_ref, d_ref, *refs):
    count = count_of(n, mode)
    out_refs, (g_buf, d_buf, sem) = refs[:count], refs[count:]
    total = rows * n
    half = total // 2
    pieces = [slice(0, half), slice(half, total)]
    copies = [
        (pltpu.make_async_copy(g_ref.at[p, :], g_buf.at[p, :], sem.at[0, i]),
         pltpu.make_async_copy(d_ref.at[p, :], d_buf.at[p, :], sem.at[1, i]))
        for i, p in enumerate(pieces)
    ]
    for pair in copies:
        for copy in pair:
            copy.start()
    matrix = split_matrix(lax.axis_index("seq"), rows, n, major(n, mode))
    for p, pair in zip(pieces, copies):
        for copy in pair:
            copy.wait()
        g_buf[p, :] = (g_buf[p, :].astype(WIDE) * d_buf[p, :].astype(WIDE)).astype(NARROW)
    span = n // count * rows
    for o in range(count):
        out_refs[o][...] = dot(matrix[o * span : (o + 1) * span, :], g_buf[...], ((1,), (0,))).astype(NARROW)


def gated_slabs(gate_in, cotangent, mode):
    rows, n, channels = gate_in.shape
    total = rows * n
    count = count_of(n, mode)
    span = n // count * rows
    out = pl.pallas_call(
        functools.partial(gated_kernel, n, mode, rows),
        in_specs=[pl.BlockSpec(memory_space=ANY)] * 2,
        out_specs=[pl.BlockSpec(memory_space=VMEM)] * count,
        out_shape=[jax.ShapeDtypeStruct((span, channels), NARROW)] * count,
        scratch_shapes=[VMEM((total, channels), NARROW)] * 2 + [pltpu.SemaphoreType.DMA((2, 2))],
        compiler_params=params(58),
        cost_estimate=cost(2 * total * total * channels, 6 * total * channels),
        name="gated_slabs",
    )(gate_in.reshape(total, channels), cotangent.reshape(total, channels))
    return [o.reshape(n // count, rows, channels) for o in out]


def inner_kernel(mode, merges, group, w_ref, x_ref, *refs):
    n, length = w_ref.shape[1:]
    count = count_of(n, mode)
    out_refs, (kept_a, kept_b, *merge_refs, kept, sem) = refs[:count], refs[count:]
    rows = group * length
    blocks = w_ref.shape[0]
    steps = blocks // group // 2

    def fetch(i, kept_x, base):
        here = pl.ds(pl.multiple_of(i * rows, rows), rows)
        there = pl.ds(pl.multiple_of((base + i) * rows, rows), rows)
        return pltpu.make_async_copy(x_ref.at[there, :], kept_x.at[here, :], sem.at[base + i])

    parts = ((kept_a, 0), (kept_b, steps))
    for kept_x, base in parts:
        for i in range(steps):
            fetch(i, kept_x, base).start()
    rank = lax.axis_index("seq")
    matrix = split_matrix(rank, blocks, n, major(n, mode))
    for merge_mode, merge_ref in zip(merges, merge_refs):
        merge_ref[...] = merge_matrix(rank, blocks, n, major(n, merge_mode))
    for kept_x, base in parts:

        def step(i, carry, kept_x=kept_x, base=base):
            fetch(i, kept_x, base).wait()
            for g in range(group):
                block = (base + i) * group + g
                x = kept_x[pl.ds(pl.multiple_of((i * group + g) * length, length), length), :]
                u = dot(w_ref[block], x, ((1,), (0,)))
                kept[pl.ds(pl.multiple_of(block * n, n), n), :] = u.astype(NARROW)
            return carry

        lax.fori_loop(0, steps, step, 0)
    span = n // count * blocks
    for o in range(count):
        out_refs[o][...] = dot(matrix[o * span : (o + 1) * span, :], kept[...], ((1,), (0,))).astype(NARROW)


def inner_slabs(first_factor, values, mode, merges):
    blocks, n, length = first_factor.shape
    channels = values.shape[1]
    group = 2 if blocks % 4 == 0 else 1
    count = count_of(n, mode)
    span = n // count * blocks
    half = VMEM((blocks // 2 * length, channels), NARROW)
    total = blocks * n
    *out, kept_a, kept_b, near, far = pl.pallas_call(
        functools.partial(inner_kernel, mode, merges, group),
        in_specs=[pl.BlockSpec(memory_space=VMEM), pl.BlockSpec(memory_space=ANY)],
        out_specs=[pl.BlockSpec(memory_space=VMEM)] * (count + 4),
        out_shape=[jax.ShapeDtypeStruct((span, channels), NARROW)] * count + [half] * 2
        + [jax.ShapeDtypeStruct((total, total), NARROW)] * 2,
        scratch_shapes=[VMEM((blocks * n, channels), NARROW), pltpu.SemaphoreType.DMA((blocks // group,))],
        compiler_params=params(20),
        cost_estimate=cost(2 * blocks * n * length * channels, 2 * blocks * length * channels),
        name="inner_slabs",
    )(first_factor, values)
    return [o.reshape(n // count, blocks, channels) for o in out], [kept_a, kept_b], near, far


def mix_kernel(n, arrive, leave, transpose, s_ref, *refs):
    (arrive_mode, arrive_parts), (leave_mode, leave_parts) = arrive, leave
    arrive_n = count_of(n, arrive_mode)
    leave_n = count_of(n, leave_mode)
    in_refs = refs[: arrive_n * arrive_parts]
    out_refs = refs[arrive_n * arrive_parts :][: leave_n * leave_parts]
    whole_ref, product = refs[arrive_n * arrive_parts + leave_n * leave_parts :]
    rank = lax.axis_index("seq")
    rows = whole_ref.shape[0] // n

    def place(group, member, mode, part, parts):
        k = number(mode, group, member)
        size = rows // parts
        return pl.ds(pl.multiple_of((rank ^ k) * rows + part * size, size), size)

    for p in range(arrive_parts):
        for a in range(arrive_n):
            for b in range(n // arrive_n):
                whole_ref[place(a, b, arrive_mode, p, arrive_parts), :] = in_refs[p * arrive_n + a][b]
    product[...] = dot(s_ref[0], whole_ref[...], ((0 if transpose else 1,), (0,))).astype(NARROW)
    for p in range(leave_parts):
        for a in range(leave_n):
            for b in range(n // leave_n):
                out_refs[p * leave_n + a][b] = product[place(a, b, leave_mode, p, leave_parts), :]


def mix(second_factor, slabs, n, arrive, leave, transpose, name):
    total = second_factor.shape[1]
    channels = slabs[0][0].shape[2]
    leave_n = count_of(n, leave[0])
    part = total // n // leave[1]
    flat = [s for half in slabs for s in half]
    out = pl.pallas_call(
        functools.partial(mix_kernel, n, arrive, leave, transpose),
        in_specs=[pl.BlockSpec(memory_space=VMEM)] * (1 + len(flat)),
        out_specs=[pl.BlockSpec(memory_space=VMEM)] * (leave_n * leave[1] + 1),
        out_shape=[jax.ShapeDtypeStruct((n // leave_n, part, channels), NARROW)] * (leave_n * leave[1])
        + [jax.ShapeDtypeStruct((total, channels), NARROW)],
        scratch_shapes=[VMEM((total, channels), NARROW)],
        compiler_params=params(10),
        cost_estimate=cost(2 * total * total * channels, 4 * total * channels),
        name=name,
    )(second_factor, *flat)
    return [out[p * leave_n : (p + 1) * leave_n] for p in range(leave[1])], out[-1]


def grads_kernel(mode, slots, group, half, held, w_ref, matrix_ref, *refs):
    n, length = w_ref.shape[1:]
    x_refs, refs = refs[:held], refs[held:]
    count = count_of(n, mode)
    slab_refs = refs[:count]
    refs = refs[count:] if half == 0 else refs[count + 2 :]
    vg_ref, fg_ref, slabs, back, fg_buf, out_buf, out_sem, fg_sem = refs
    part = slab_refs[0].shape[1]
    base = half * part
    steps = part // group
    rows = group * length

    def put(i, s):
        there = pl.ds(pl.multiple_of(base * length + i * rows, rows), rows)
        return pltpu.make_async_copy(out_buf.at[s], vg_ref.at[there, :], out_sem.at[s])

    every = n // count
    for o in range(count):
        for b in range(every):
            slabs[(o * every + b) * part : (o * every + b + 1) * part, :] = slab_refs[o][b]
    if matrix_ref.shape[0] == slabs.shape[0]:
        matrix = matrix_ref[...]
    else:
        matrix = merge_matrix(lax.axis_index("seq"), part, n, major(n, mode))
    back[...] = dot(matrix, slabs[...], ((1,), (0,))).astype(NARROW)

    each = steps // held

    def step(x_ref, start, i, carry):
        s = lax.rem(i, slots)

        @pl.when(i >= slots)
        def _():
            put(i - slots, s).wait()

        for g in range(group):
            block = i * group + g
            w = w_ref[base + block]
            f = back[pl.ds(pl.multiple_of(block * n, n), n), :]
            out_buf[s, g * length : (g + 1) * length, :] = dot(w, f, ((0,), (0,))).astype(NARROW)
            x = x_ref[pl.ds(pl.multiple_of((block - start * group) * length, length), length), :]
            fg_buf[block] = dot(f, x, ((1,), (1,))).astype(NARROW)
        put(i, s).start()
        return carry

    for h in range(held):
        lax.fori_loop(h * each, (h + 1) * each, functools.partial(step, x_refs[h], h * each), 0)
    last = pltpu.make_async_copy(fg_buf, fg_ref.at[pl.ds(base, part)], fg_sem)
    last.start()
    for i in range(steps - slots, steps):
        put(i, i % slots).wait()
    last.wait()


def grads(first_factor, matrix, kept_x, slabs, mode, half, earlier):
    blocks, n, length = first_factor.shape
    channels = kept_x[0].shape[1]
    held, count = len(kept_x), len(slabs)
    part = slabs[0].shape[1]
    group = next(g for g in (4, 2, 1) if part % g == 0)
    slots = min(3, part // group)
    shapes = [
        jax.ShapeDtypeStruct((blocks * length, channels), NARROW),
        jax.ShapeDtypeStruct(first_factor.shape, NARROW),
    ]
    return pl.pallas_call(
        functools.partial(grads_kernel, mode, slots, group, half, held),
        in_specs=[pl.BlockSpec(memory_space=VMEM)] * (2 + held + count)
        + ([] if half == 0 else [pl.BlockSpec(memory_space=ANY)] * 2),
        out_specs=[pl.BlockSpec(memory_space=ANY)] * 2,
        out_shape=shapes,
        input_output_aliases={} if half == 0 else {2 + held + count: 0, 3 + held + count: 1},
        scratch_shapes=[
            VMEM((part * n, channels), NARROW),
            VMEM((part * n, channels), NARROW),
            VMEM((part, n, length), NARROW),
            VMEM((slots, group * length, channels), NARROW),
            pltpu.SemaphoreType.DMA((slots,)),
            pltpu.SemaphoreType.DMA,
        ],
        compiler_params=params(16),
        cost_estimate=cost(4 * part * n * length * channels, 2 * part * length * channels),
        name="grads",
    )(first_factor, matrix, *kept_x, *slabs, *(earlier or ()))


def gates_kernel(n, mode, pieces, matrix_ref, g_ref, d_ref, *refs):
    count = count_of(n, mode)
    slab_refs, (mixed_ref, grad_ref, slabs, mixed, grad, sem) = refs[:count], refs[count:]
    span = slab_refs[0].shape[0]
    for o in range(count):
        slabs[o * span : (o + 1) * span, :] = slab_refs[o][...]
    size = slabs.shape[0] // pieces
    copies = []
    for p in range(pieces):
        here = slice(p * size, (p + 1) * size)
        z = dot(matrix_ref[here, :], slabs[...], ((1,), (0,)))
        mixed[here, :] = (g_ref[here, :].astype(WIDE) * z).astype(NARROW)
        grad[here, :] = (d_ref[here, :].astype(WIDE) * z).astype(NARROW)
        copies.append(pltpu.make_async_copy(mixed.at[here, :], mixed_ref.at[here, :], sem.at[0, p]))
        copies.append(pltpu.make_async_copy(grad.at[here, :], grad_ref.at[here, :], sem.at[1, p]))
        copies[-2].start()
        copies[-1].start()
    for copy in copies:
        copy.wait()


def gates(matrix, gate_in, cotangent, slabs, mode):
    rows, n, channels = gate_in.shape
    total = rows * n
    count = count_of(n, mode)
    span = n // count * rows
    pieces = 2
    out = pl.pallas_call(
        functools.partial(gates_kernel, n, mode, pieces),
        in_specs=[pl.BlockSpec(memory_space=VMEM)] * (3 + count),
        out_specs=[pl.BlockSpec(memory_space=ANY)] * 2,
        out_shape=[jax.ShapeDtypeStruct((total, channels), NARROW)] * 2,
        scratch_shapes=[VMEM((total, channels), NARROW)] * 3 + [pltpu.SemaphoreType.DMA((2, pieces))],
        compiler_params=params(10),
        cost_estimate=cost(2 * total * total * channels, 10 * total * channels),
        name="gates",
    )(
        matrix,
        gate_in.reshape(total, channels),
        cotangent.reshape(total, channels),
        *[s.reshape(span, channels) for s in slabs],
    )
    return [o.reshape(gate_in.shape) for o in out]


def after(arrays, *tokens):
    return list(lax.optimization_barrier(tuple(arrays) + tokens)[: len(arrays)])


def regroup(slabs):
    count = slabs[0].shape[0]
    return [jnp.stack([s[b] for s in slabs]) for b in range(count)]


def by_permutes(values, gate_in, cotangent, first_factor, second_factor, inner):
    n = gate_in.shape[1]
    near, far = (True, inner), (False, inner)

    def permutes(slabs, step):
        got = list(slabs)
        count = len(slabs)
        for k in [2, 3, 1] if count == 4 else range(count - 1, 0, -1):
            got[k] = lax.ppermute(slabs[k], "seq", [(i, i ^ (k * step)) for i in range(n)])
        return got

    def across(slabs):
        return permutes(slabs, inner)

    def beside(slabs):
        return permutes(slabs, 1)

    gated = gated_slabs(gate_in, cotangent, far)
    e = across(gated)
    (factor,) = after([first_factor], gated[0])
    u, kept_x, merge_near, merge_far = inner_slabs(factor, values, far, (near, far))
    e = beside(regroup(after(e, u[0])))
    u = across(u)
    (f,), e_all = mix(second_factor, [e], n, (near, 1), (far, 1), True, "back")
    f = across(f)
    u = beside(regroup(u))
    (z,), u_all = mix(second_factor, [u], n, (near, 1), (near, 1), False, "forth")
    z = across(regroup(beside(z)))
    f = beside(regroup(f))
    values_grad, first_grad = grads(first_factor, merge_near, kept_x, f, near, 0, None)
    second_grad = dot(e_all, u_all, ((1,), (1,))).astype(NARROW)[None]
    gate_in, cotangent = after([gate_in, cotangent], first_grad)
    mixed, gate_grad = gates(merge_far, gate_in, cotangent, z, far)
    return mixed, values_grad, gate_grad, first_grad, second_grad


def by_all_to_all(values, gate_in, cotangent, first_factor, second_factor):
    block_len = first_factor.shape[2]
    channels = values.shape[1]
    blocks_x = values.reshape(-1, block_len, channels)
    inner = jnp.einsum("aqp,apc->aqc", first_factor, blocks_x, preferred_element_type=WIDE).astype(NARROW)
    gated = (gate_in.astype(WIDE) * cotangent.astype(WIDE)).astype(NARROW)
    inner_t = lax.all_to_all(inner, "seq", split_axis=1, concat_axis=0, tiled=True)
    outer_t = jnp.einsum("qxa,aqc->xqc", second_factor, inner_t, preferred_element_type=WIDE).astype(NARROW)
    outer = lax.all_to_all(outer_t, "seq", split_axis=0, concat_axis=1, tiled=True)
    gated_t = lax.all_to_all(gated, "seq", split_axis=1, concat_axis=0, tiled=True)
    second_grad = jnp.einsum("xqc,aqc->qxa", gated_t, inner_t, preferred_element_type=WIDE).astype(NARROW)
    back_t = jnp.einsum("qxa,xqc->aqc", second_factor, gated_t, preferred_element_type=WIDE).astype(NARROW)
    back_inner = lax.all_to_all(back_t, "seq", split_axis=0, concat_axis=1, tiled=True)
    outer_f = outer.astype(WIDE)
    mixed = (gate_in.astype(WIDE) * outer_f).astype(NARROW)
    gate_grad = (cotangent.astype(WIDE) * outer_f).astype(NARROW)
    first_grad = jnp.einsum("aqc,apc->aqp", back_inner, blocks_x, preferred_element_type=WIDE).astype(NARROW)
    values_grad = (
        jnp.einsum("aqp,aqc->apc", first_factor, back_inner, preferred_element_type=WIDE)
        .astype(NARROW)
        .reshape(-1, channels)
    )
    return mixed, values_grad, gate_grad, first_grad, second_grad


def solution(mesh):
    n = mesh.shape["seq"]

    def on_device(values, gate_in, cotangent, first_factor, second_factor):
        rows, kept = gate_in.shape[:2]
        if n == 16 and kept == n and rows % 32 == 0 and first_factor.shape[0] == rows:
            return by_permutes(values, gate_in, cotangent, first_factor, second_factor, 4)
        return by_all_to_all(values, gate_in, cotangent, first_factor, second_factor)

    both = ("grp", "seq")
    return jax.shard_map(
        on_device,
        mesh=mesh,
        in_specs=(
            P(both, None),
            P(both, None, None),
            P(both, None, None),
            P("seq", None, None),
            P("seq", None, None),
        ),
        out_specs=(
            P(both, None, None),
            P(both, None),
            P(both, None, None),
            P(both, None, None),
            P(both, None, None),
        ),
        check_vma=False,
    )
```

```python
import functools

import jax
import jax.numpy as jnp
from jax import lax
from jax.experimental import pallas as pl
from jax.experimental.pallas import tpu as pltpu
from jax.sharding import PartitionSpec as P

WIDE = jnp.float32
NARROW = jnp.bfloat16
MIB = 1 << 20
VMEM = pltpu.VMEM
ANY = pltpu.HBM


def params(mib):
    return pltpu.CompilerParams(vmem_limit_bytes=mib * MIB)


def cost(flops, nbytes):
    return pl.CostEstimate(flops=flops, bytes_accessed=nbytes, transcendentals=0)


def split_matrix(rank, rows, n, order):
    total = rows * n
    shape = (total, total)
    i = lax.broadcasted_iota(jnp.int32, shape, 0)
    j = lax.broadcasted_iota(jnp.int32, shape, 1)
    slab, block = i // rows, i % rows
    k = order(slab)
    return ((j // n == block) & (j % n == (rank ^ k))).astype(NARROW)


def merge_matrix(rank, rows, n, order):
    total = rows * n
    shape = (total, total)
    i = lax.broadcasted_iota(jnp.int32, shape, 0)
    j = lax.broadcasted_iota(jnp.int32, shape, 1)
    slab, block = j // rows, j % rows
    k = order(slab)
    return ((i // n == block) & (i % n == (rank ^ k))).astype(NARROW)


def count_of(n, mode):
    by_inner, inner = mode
    return inner if by_inner else n // inner


ORDER = (0, 2, 3, 1)


def partner(place):
    if isinstance(place, int):
        return ORDER[place]
    return sum(jnp.where(place == i, k, 0) for i, k in enumerate(ORDER))


def number(mode, group, member):
    by_inner, inner = mode
    high, low = (member, group) if by_inner else (group, member)
    return partner(high) * inner + partner(low)


def major(n, mode):
    each = n // count_of(n, mode)
    return lambda place: number(mode, place // each, place % each)


def dot(a, b, dims):
    return lax.dot_general(a, b, (dims, ((), ())), preferred_element_type=WIDE)


def gated_kernel(n, mode, rows, g_ref, d_ref, *refs):
    count = count_of(n, mode)
    out_refs, (g_buf, d_buf, sem) = refs[:count], refs[count:]
    total = rows * n
    half = total // 2
    pieces = [slice(0, half), slice(half, total)]
    copies = [
        (pltpu.make_async_copy(g_ref.at[p, :], g_buf.at[p, :], sem.at[0, i]),
         pltpu.make_async_copy(d_ref.at[p, :], d_buf.at[p, :], sem.at[1, i]))
        for i, p in enumerate(pieces)
    ]
    for pair in copies:
        for copy in pair:
            copy.start()
    matrix = split_matrix(lax.axis_index("seq"), rows, n, major(n, mode))
    for p, pair in zip(pieces, copies):
        for copy in pair:
            copy.wait()
        g_buf[p, :] = (g_buf[p, :].astype(WIDE) * d_buf[p, :].astype(WIDE)).astype(NARROW)
    span = n // count * rows
    for o in range(count):
        out_refs[o][...] = dot(matrix[o * span : (o + 1) * span, :], g_buf[...], ((1,), (0,))).astype(NARROW)


def gated_slabs(gate_in, cotangent, mode):
    rows, n, channels = gate_in.shape
    total = rows * n
    count = count_of(n, mode)
    span = n // count * rows
    out = pl.pallas_call(
        functools.partial(gated_kernel, n, mode, rows),
        in_specs=[pl.BlockSpec(memory_space=ANY)] * 2,
        out_specs=[pl.BlockSpec(memory_space=VMEM)] * count,
        out_shape=[jax.ShapeDtypeStruct((span, channels), NARROW)] * count,
        scratch_shapes=[VMEM((total, channels), NARROW)] * 2 + [pltpu.SemaphoreType.DMA((2, 2))],
        compiler_params=params(58),
        cost_estimate=cost(2 * total * total * channels, 6 * total * channels),
        name="gated_slabs",
    )(gate_in.reshape(total, channels), cotangent.reshape(total, channels))
    return [o.reshape(n // count, rows, channels) for o in out]


def inner_kernel(mode, merges, group, w_ref, x_ref, *refs):
    n, length = w_ref.shape[1:]
    count = count_of(n, mode)
    out_refs, (kept_a, kept_b, *merge_refs, kept, sem) = refs[:count], refs[count:]
    rows = group * length
    blocks = w_ref.shape[0]
    steps = blocks // group // 2

    def fetch(i, kept_x, base):
        here = pl.ds(pl.multiple_of(i * rows, rows), rows)
        there = pl.ds(pl.multiple_of((base + i) * rows, rows), rows)
        return pltpu.make_async_copy(x_ref.at[there, :], kept_x.at[here, :], sem.at[base + i])

    parts = ((kept_a, 0), (kept_b, steps))
    for kept_x, base in parts:
        for i in range(steps):
            fetch(i, kept_x, base).start()
    rank = lax.axis_index("seq")
    matrix = split_matrix(rank, blocks, n, major(n, mode))
    for merge_mode, merge_ref in zip(merges, merge_refs):
        merge_ref[...] = merge_matrix(rank, blocks, n, major(n, merge_mode))
    for kept_x, base in parts:

        def step(i, carry, kept_x=kept_x, base=base):
            fetch(i, kept_x, base).wait()
            for g in range(group):
                block = (base + i) * group + g
                x = kept_x[pl.ds(pl.multiple_of((i * group + g) * length, length), length), :]
                u = dot(w_ref[block], x, ((1,), (0,)))
                kept[pl.ds(pl.multiple_of(block * n, n), n), :] = u.astype(NARROW)
            return carry

        lax.fori_loop(0, steps, step, 0)
    span = n // count * blocks
    for o in range(count):
        out_refs[o][...] = dot(matrix[o * span : (o + 1) * span, :], kept[...], ((1,), (0,))).astype(NARROW)


def inner_slabs(first_factor, values, mode, merges):
    blocks, n, length = first_factor.shape
    channels = values.shape[1]
    group = 2 if blocks % 4 == 0 else 1
    count = count_of(n, mode)
    span = n // count * blocks
    half = VMEM((blocks // 2 * length, channels), NARROW)
    total = blocks * n
    *out, kept_a, kept_b, near, far = pl.pallas_call(
        functools.partial(inner_kernel, mode, merges, group),
        in_specs=[pl.BlockSpec(memory_space=VMEM), pl.BlockSpec(memory_space=ANY)],
        out_specs=[pl.BlockSpec(memory_space=VMEM)] * (count + 4),
        out_shape=[jax.ShapeDtypeStruct((span, channels), NARROW)] * count + [half] * 2
        + [jax.ShapeDtypeStruct((total, total), NARROW)] * 2,
        scratch_shapes=[VMEM((blocks * n, channels), NARROW), pltpu.SemaphoreType.DMA((blocks // group,))],
        compiler_params=params(20),
        cost_estimate=cost(2 * blocks * n * length * channels, 2 * blocks * length * channels),
        name="inner_slabs",
    )(first_factor, values)
    return [o.reshape(n // count, blocks, channels) for o in out], [kept_a, kept_b], near, far


def mix_kernel(n, arrive, leave, transpose, s_ref, *refs):
    (arrive_mode, arrive_parts), (leave_mode, leave_parts) = arrive, leave
    arrive_n = count_of(n, arrive_mode)
    leave_n = count_of(n, leave_mode)
    in_refs = refs[: arrive_n * arrive_parts]
    out_refs = refs[arrive_n * arrive_parts :][: leave_n * leave_parts]
    whole_ref, product = refs[arrive_n * arrive_parts + leave_n * leave_parts :]
    rank = lax.axis_index("seq")
    rows = whole_ref.shape[0] // n

    def place(group, member, mode, part, parts):
        k = number(mode, group, member)
        size = rows // parts
        return pl.ds(pl.multiple_of((rank ^ k) * rows + part * size, size), size)

    for p in range(arrive_parts):
        for a in range(arrive_n):
            for b in range(n // arrive_n):
                whole_ref[place(a, b, arrive_mode, p, arrive_parts), :] = in_refs[p * arrive_n + a][b]
    product[...] = dot(s_ref[0], whole_ref[...], ((0 if transpose else 1,), (0,))).astype(NARROW)
    for p in range(leave_parts):
        for a in range(leave_n):
            for b in range(n // leave_n):
                out_refs[p * leave_n + a][b] = product[place(a, b, leave_mode, p, leave_parts), :]


def mix(second_factor, slabs, n, arrive, leave, transpose, name):
    total = second_factor.shape[1]
    channels = slabs[0][0].shape[2]
    leave_n = count_of(n, leave[0])
    part = total // n // leave[1]
    flat = [s for half in slabs for s in half]
    out = pl.pallas_call(
        functools.partial(mix_kernel, n, arrive, leave, transpose),
        in_specs=[pl.BlockSpec(memory_space=VMEM)] * (1 + len(flat)),
        out_specs=[pl.BlockSpec(memory_space=VMEM)] * (leave_n * leave[1] + 1),
        out_shape=[jax.ShapeDtypeStruct((n // leave_n, part, channels), NARROW)] * (leave_n * leave[1])
        + [jax.ShapeDtypeStruct((total, channels), NARROW)],
        scratch_shapes=[VMEM((total, channels), NARROW)],
        compiler_params=params(10),
        cost_estimate=cost(2 * total * total * channels, 4 * total * channels),
        name=name,
    )(second_factor, *flat)
    return [out[p * leave_n : (p + 1) * leave_n] for p in range(leave[1])], out[-1]


def grads_kernel(mode, slots, group, half, held, w_ref, matrix_ref, *refs):
    n, length = w_ref.shape[1:]
    x_refs, refs = refs[:held], refs[held:]
    count = count_of(n, mode)
    slab_refs = refs[:count]
    refs = refs[count:] if half == 0 else refs[count + 2 :]
    vg_ref, fg_ref, slabs, back, fg_buf, out_buf, out_sem, fg_sem = refs
    part = slab_refs[0].shape[1]
    base = half * part
    steps = part // group
    rows = group * length

    def put(i, s):
        there = pl.ds(pl.multiple_of(base * length + i * rows, rows), rows)
        return pltpu.make_async_copy(out_buf.at[s], vg_ref.at[there, :], out_sem.at[s])

    every = n // count
    for o in range(count):
        for b in range(every):
            slabs[(o * every + b) * part : (o * every + b + 1) * part, :] = slab_refs[o][b]
    if matrix_ref.shape[0] == slabs.shape[0]:
        matrix = matrix_ref[...]
    else:
        matrix = merge_matrix(lax.axis_index("seq"), part, n, major(n, mode))
    back[...] = dot(matrix, slabs[...], ((1,), (0,))).astype(NARROW)

    each = steps // held

    def step(x_ref, start, i, carry):
        s = lax.rem(i, slots)

        @pl.when(i >= slots)
        def _():
            put(i - slots, s).wait()

        for g in range(group):
            block = i * group + g
            w = w_ref[base + block]
            f = back[pl.ds(pl.multiple_of(block * n, n), n), :]
            out_buf[s, g * length : (g + 1) * length, :] = dot(w, f, ((0,), (0,))).astype(NARROW)
            x = x_ref[pl.ds(pl.multiple_of((block - start * group) * length, length), length), :]
            fg_buf[block] = dot(f, x, ((1,), (1,))).astype(NARROW)
        put(i, s).start()
        return carry

    for h in range(held):
        lax.fori_loop(h * each, (h + 1) * each, functools.partial(step, x_refs[h], h * each), 0)
    last = pltpu.make_async_copy(fg_buf, fg_ref.at[pl.ds(base, part)], fg_sem)
    last.start()
    for i in range(steps - slots, steps):
        put(i, i % slots).wait()
    last.wait()


def grads(first_factor, matrix, kept_x, slabs, mode, half, earlier):
    blocks, n, length = first_factor.shape
    channels = kept_x[0].shape[1]
    held, count = len(kept_x), len(slabs)
    part = slabs[0].shape[1]
    group = next(g for g in (4, 2, 1) if part % g == 0)
    slots = min(3, part // group)
    shapes = [
        jax.ShapeDtypeStruct((blocks * length, channels), NARROW),
        jax.ShapeDtypeStruct(first_factor.shape, NARROW),
    ]
    return pl.pallas_call(
        functools.partial(grads_kernel, mode, slots, group, half, held),
        in_specs=[pl.BlockSpec(memory_space=VMEM)] * (2 + held + count)
        + ([] if half == 0 else [pl.BlockSpec(memory_space=ANY)] * 2),
        out_specs=[pl.BlockSpec(memory_space=ANY)] * 2,
        out_shape=shapes,
        input_output_aliases={} if half == 0 else {2 + held + count: 0, 3 + held + count: 1},
        scratch_shapes=[
            VMEM((part * n, channels), NARROW),
            VMEM((part * n, channels), NARROW),
            VMEM((part, n, length), NARROW),
            VMEM((slots, group * length, channels), NARROW),
            pltpu.SemaphoreType.DMA((slots,)),
            pltpu.SemaphoreType.DMA,
        ],
        compiler_params=params(16),
        cost_estimate=cost(4 * part * n * length * channels, 2 * part * length * channels),
        name="grads",
    )(first_factor, matrix, *kept_x, *slabs, *(earlier or ()))


def gates_kernel(n, mode, pieces, matrix_ref, g_ref, d_ref, *refs):
    count = count_of(n, mode)
    slab_refs, (mixed_ref, grad_ref, slabs, mixed, grad, sem) = refs[:count], refs[count:]
    span = slab_refs[0].shape[0]
    for o in range(count):
        slabs[o * span : (o + 1) * span, :] = slab_refs[o][...]
    size = slabs.shape[0] // pieces
    copies = []
    for p in range(pieces):
        here = slice(p * size, (p + 1) * size)
        z = dot(matrix_ref[here, :], slabs[...], ((1,), (0,)))
        mixed[here, :] = (g_ref[here, :].astype(WIDE) * z).astype(NARROW)
        grad[here, :] = (d_ref[here, :].astype(WIDE) * z).astype(NARROW)
        copies.append(pltpu.make_async_copy(mixed.at[here, :], mixed_ref.at[here, :], sem.at[0, p]))
        copies.append(pltpu.make_async_copy(grad.at[here, :], grad_ref.at[here, :], sem.at[1, p]))
        copies[-2].start()
        copies[-1].start()
    for copy in copies:
        copy.wait()


def gates(matrix, gate_in, cotangent, slabs, mode):
    rows, n, channels = gate_in.shape
    total = rows * n
    count = count_of(n, mode)
    span = n // count * rows
    pieces = 2
    out = pl.pallas_call(
        functools.partial(gates_kernel, n, mode, pieces),
        in_specs=[pl.BlockSpec(memory_space=VMEM)] * (3 + count),
        out_specs=[pl.BlockSpec(memory_space=ANY)] * 2,
        out_shape=[jax.ShapeDtypeStruct((total, channels), NARROW)] * 2,
        scratch_shapes=[VMEM((total, channels), NARROW)] * 3 + [pltpu.SemaphoreType.DMA((2, pieces))],
        compiler_params=params(10),
        cost_estimate=cost(2 * total * total * channels, 10 * total * channels),
        name="gates",
    )(
        matrix,
        gate_in.reshape(total, channels),
        cotangent.reshape(total, channels),
        *[s.reshape(span, channels) for s in slabs],
    )
    return [o.reshape(gate_in.shape) for o in out]


def after(arrays, *tokens):
    return list(lax.optimization_barrier(tuple(arrays) + tokens)[: len(arrays)])


def regroup(slabs):
    count = slabs[0].shape[0]
    return [jnp.stack([s[b] for s in slabs]) for b in range(count)]


def by_permutes(values, gate_in, cotangent, first_factor, second_factor, inner):
    n = gate_in.shape[1]
    near, far = (True, inner), (False, inner)

    def permutes(slabs, step):
        got = list(slabs)
        for i in range(1, len(slabs)):
            got[i] = lax.ppermute(slabs[i], "seq", [(j, j ^ (ORDER[i] * step)) for j in range(n)])
        return got

    def across(slabs):
        return permutes(slabs, inner)

    def beside(slabs):
        return permutes(slabs, 1)

    gated = gated_slabs(gate_in, cotangent, far)
    e = across(gated)
    (factor,) = after([first_factor], gated[0])
    u, kept_x, merge_near, merge_far = inner_slabs(factor, values, far, (near, far))
    e = beside(regroup(after(e, u[0])))
    u = across(u)
    (f,), e_all = mix(second_factor, [e], n, (near, 1), (far, 1), True, "back")
    f = across(f)
    u = beside(regroup(u))
    (z,), u_all = mix(second_factor, [u], n, (near, 1), (near, 1), False, "forth")
    z = across(regroup(beside(z)))
    f = beside(regroup(f))
    values_grad, first_grad = grads(first_factor, merge_near, kept_x, f, near, 0, None)
    second_grad = dot(e_all, u_all, ((1,), (1,))).astype(NARROW)[None]
    gate_in, cotangent = after([gate_in, cotangent], first_grad)
    mixed, gate_grad = gates(merge_far, gate_in, cotangent, z, far)
    return mixed, values_grad, gate_grad, first_grad, second_grad


def by_all_to_all(values, gate_in, cotangent, first_factor, second_factor):
    block_len = first_factor.shape[2]
    channels = values.shape[1]
    blocks_x = values.reshape(-1, block_len, channels)
    inner = jnp.einsum("aqp,apc->aqc", first_factor, blocks_x, preferred_element_type=WIDE).astype(NARROW)
    gated = (gate_in.astype(WIDE) * cotangent.astype(WIDE)).astype(NARROW)
    inner_t = lax.all_to_all(inner, "seq", split_axis=1, concat_axis=0, tiled=True)
    outer_t = jnp.einsum("qxa,aqc->xqc", second_factor, inner_t, preferred_element_type=WIDE).astype(NARROW)
    outer = lax.all_to_all(outer_t, "seq", split_axis=0, concat_axis=1, tiled=True)
    gated_t = lax.all_to_all(gated, "seq", split_axis=1, concat_axis=0, tiled=True)
    second_grad = jnp.einsum("xqc,aqc->qxa", gated_t, inner_t, preferred_element_type=WIDE).astype(NARROW)
    back_t = jnp.einsum("qxa,xqc->aqc", second_factor, gated_t, preferred_element_type=WIDE).astype(NARROW)
    back_inner = lax.all_to_all(back_t, "seq", split_axis=0, concat_axis=1, tiled=True)
    outer_f = outer.astype(WIDE)
    mixed = (gate_in.astype(WIDE) * outer_f).astype(NARROW)
    gate_grad = (cotangent.astype(WIDE) * outer_f).astype(NARROW)
    first_grad = jnp.einsum("aqc,apc->aqp", back_inner, blocks_x, preferred_element_type=WIDE).astype(NARROW)
    values_grad = (
        jnp.einsum("aqp,aqc->apc", first_factor, back_inner, preferred_element_type=WIDE)
        .astype(NARROW)
        .reshape(-1, channels)
    )
    return mixed, values_grad, gate_grad, first_grad, second_grad


def solution(mesh):
    n = mesh.shape["seq"]

    def on_device(values, gate_in, cotangent, first_factor, second_factor):
        rows, kept = gate_in.shape[:2]
        if n == 16 and kept == n and rows % 32 == 0 and first_factor.shape[0] == rows:
            return by_permutes(values, gate_in, cotangent, first_factor, second_factor, 4)
        return by_all_to_all(values, gate_in, cotangent, first_factor, second_factor)

    both = ("grp", "seq")
    return jax.shard_map(
        on_device,
        mesh=mesh,
        in_specs=(
            P(both, None),
            P(both, None, None),
            P(both, None, None),
            P("seq", None, None),
            P("seq", None, None),
        ),
        out_specs=(
            P(both, None, None),
            P(both, None),
            P(both, None, None),
            P(both, None, None),
            P(both, None, None),
        ),
        check_vma=False,
    )
```

```python
import functools

import jax
import jax.numpy as jnp
from jax import lax
from jax.experimental import pallas as pl
from jax.experimental.pallas import tpu as pltpu
from jax.sharding import PartitionSpec as P

WIDE = jnp.float32
NARROW = jnp.bfloat16
MIB = 1 << 20
VMEM = pltpu.VMEM
ANY = pltpu.HBM


def params(mib):
    return pltpu.CompilerParams(vmem_limit_bytes=mib * MIB)


def cost(flops, nbytes):
    return pl.CostEstimate(flops=flops, bytes_accessed=nbytes, transcendentals=0)


def split_matrix(rank, rows, n, order):
    total = rows * n
    shape = (total, total)
    i = lax.broadcasted_iota(jnp.int32, shape, 0)
    j = lax.broadcasted_iota(jnp.int32, shape, 1)
    slab, block = i // rows, i % rows
    k = order(slab)
    return ((j // n == block) & (j % n == (rank ^ k))).astype(NARROW)


def merge_matrix(rank, rows, n, order):
    total = rows * n
    shape = (total, total)
    i = lax.broadcasted_iota(jnp.int32, shape, 0)
    j = lax.broadcasted_iota(jnp.int32, shape, 1)
    slab, block = j // rows, j % rows
    k = order(slab)
    return ((i // n == block) & (i % n == (rank ^ k))).astype(NARROW)


def count_of(n, mode):
    by_inner, inner = mode
    return inner if by_inner else n // inner


ORDER = (0, 2, 3, 1)


def partner(place):
    if isinstance(place, int):
        return ORDER[place]
    return sum(jnp.where(place == i, k, 0) for i, k in enumerate(ORDER))


def number(mode, group, member):
    by_inner, inner = mode
    high, low = (member, group) if by_inner else (group, member)
    return partner(high) * inner + partner(low)


def major(n, mode):
    each = n // count_of(n, mode)
    return lambda place: number(mode, place // each, place % each)


def dot(a, b, dims):
    return lax.dot_general(a, b, (dims, ((), ())), preferred_element_type=WIDE)


def gated_kernel(n, mode, rows, g_ref, d_ref, *refs):
    count = count_of(n, mode)
    out_refs, (g_buf, d_buf, sem) = refs[:count], refs[count:]
    total = rows * n
    half = total // 2
    pieces = [slice(0, half), slice(half, total)]
    copies = [
        (pltpu.make_async_copy(g_ref.at[p, :], g_buf.at[p, :], sem.at[0, i]),
         pltpu.make_async_copy(d_ref.at[p, :], d_buf.at[p, :], sem.at[1, i]))
        for i, p in enumerate(pieces)
    ]
    for pair in copies:
        for copy in pair:
            copy.start()
    matrix = split_matrix(lax.axis_index("seq"), rows, n, major(n, mode))
    for p, pair in zip(pieces, copies):
        for copy in pair:
            copy.wait()
        g_buf[p, :] = (g_buf[p, :].astype(WIDE) * d_buf[p, :].astype(WIDE)).astype(NARROW)
    span = n // count * rows
    for o in range(count):
        out_refs[o][...] = dot(matrix[o * span : (o + 1) * span, :], g_buf[...], ((1,), (0,))).astype(NARROW)


def gated_slabs(gate_in, cotangent, mode):
    rows, n, channels = gate_in.shape
    total = rows * n
    count = count_of(n, mode)
    span = n // count * rows
    out = pl.pallas_call(
        functools.partial(gated_kernel, n, mode, rows),
        in_specs=[pl.BlockSpec(memory_space=ANY)] * 2,
        out_specs=[pl.BlockSpec(memory_space=VMEM)] * count,
        out_shape=[jax.ShapeDtypeStruct((span, channels), NARROW)] * count,
        scratch_shapes=[VMEM((total, channels), NARROW)] * 2 + [pltpu.SemaphoreType.DMA((2, 2))],
        compiler_params=params(58),
        cost_estimate=cost(2 * total * total * channels, 6 * total * channels),
        name="gated_slabs",
    )(gate_in.reshape(total, channels), cotangent.reshape(total, channels))
    return [o.reshape(n // count, rows, channels) for o in out]


def inner_kernel(mode, merges, group, w_ref, x_ref, *refs):
    n, length = w_ref.shape[1:]
    count = count_of(n, mode)
    out_refs, (kept_a, kept_b, *merge_refs, kept, sem) = refs[:count], refs[count:]
    rows = group * length
    blocks = w_ref.shape[0]
    steps = blocks // group // 2

    def fetch(i, kept_x, base):
        here = pl.ds(pl.multiple_of(i * rows, rows), rows)
        there = pl.ds(pl.multiple_of((base + i) * rows, rows), rows)
        return pltpu.make_async_copy(x_ref.at[there, :], kept_x.at[here, :], sem.at[base + i])

    parts = ((kept_a, 0), (kept_b, steps))
    for kept_x, base in parts:
        for i in range(steps):
            fetch(i, kept_x, base).start()
    rank = lax.axis_index("seq")
    matrix = split_matrix(rank, blocks, n, major(n, mode))
    for merge_mode, merge_ref in zip(merges, merge_refs):
        merge_ref[...] = merge_matrix(rank, blocks, n, major(n, merge_mode))
    for kept_x, base in parts:

        def step(i, carry, kept_x=kept_x, base=base):
            fetch(i, kept_x, base).wait()
            for g in range(group):
                block = (base + i) * group + g
                x = kept_x[pl.ds(pl.multiple_of((i * group + g) * length, length), length), :]
                u = dot(w_ref[block], x, ((1,), (0,)))
                kept[pl.ds(pl.multiple_of(block * n, n), n), :] = u.astype(NARROW)
            return carry

        lax.fori_loop(0, steps, step, 0)
    span = n // count * blocks
    for o in range(count):
        out_refs[o][...] = dot(matrix[o * span : (o + 1) * span, :], kept[...], ((1,), (0,))).astype(NARROW)


def inner_slabs(first_factor, values, mode, merges):
    blocks, n, length = first_factor.shape
    channels = values.shape[1]
    group = 2 if blocks % 4 == 0 else 1
    count = count_of(n, mode)
    span = n // count * blocks
    half = VMEM((blocks // 2 * length, channels), NARROW)
    total = blocks * n
    *out, kept_a, kept_b, near, far = pl.pallas_call(
        functools.partial(inner_kernel, mode, merges, group),
        in_specs=[pl.BlockSpec(memory_space=VMEM), pl.BlockSpec(memory_space=ANY)],
        out_specs=[pl.BlockSpec(memory_space=VMEM)] * (count + 4),
        out_shape=[jax.ShapeDtypeStruct((span, channels), NARROW)] * count + [half] * 2
        + [jax.ShapeDtypeStruct((total, total), NARROW)] * 2,
        scratch_shapes=[VMEM((blocks * n, channels), NARROW), pltpu.SemaphoreType.DMA((blocks // group,))],
        compiler_params=params(20),
        cost_estimate=cost(2 * blocks * n * length * channels, 2 * blocks * length * channels),
        name="inner_slabs",
    )(first_factor, values)
    return [o.reshape(n // count, blocks, channels) for o in out], [kept_a, kept_b], near, far


def mix_kernel(n, arrive, leave, transpose, s_ref, *refs):
    (arrive_mode, arrive_parts), (leave_mode, leave_parts) = arrive, leave
    arrive_n = count_of(n, arrive_mode)
    leave_n = count_of(n, leave_mode)
    in_refs = refs[: arrive_n * arrive_parts]
    out_refs = refs[arrive_n * arrive_parts :][: leave_n * leave_parts]
    whole_ref, product = refs[arrive_n * arrive_parts + leave_n * leave_parts :]
    rank = lax.axis_index("seq")
    rows = whole_ref.shape[0] // n

    def place(group, member, mode, part, parts):
        k = number(mode, group, member)
        size = rows // parts
        return pl.ds(pl.multiple_of((rank ^ k) * rows + part * size, size), size)

    for p in range(arrive_parts):
        for a in range(arrive_n):
            for b in range(n // arrive_n):
                whole_ref[place(a, b, arrive_mode, p, arrive_parts), :] = in_refs[p * arrive_n + a][b]
    product[...] = dot(s_ref[0], whole_ref[...], ((0 if transpose else 1,), (0,))).astype(NARROW)
    for p in range(leave_parts):
        for a in range(leave_n):
            for b in range(n // leave_n):
                out_refs[p * leave_n + a][b] = product[place(a, b, leave_mode, p, leave_parts), :]


def mix(second_factor, slabs, n, arrive, leave, transpose, name):
    total = second_factor.shape[1]
    channels = slabs[0][0].shape[2]
    leave_n = count_of(n, leave[0])
    part = total // n // leave[1]
    flat = [s for half in slabs for s in half]
    out = pl.pallas_call(
        functools.partial(mix_kernel, n, arrive, leave, transpose),
        in_specs=[pl.BlockSpec(memory_space=VMEM)] * (1 + len(flat)),
        out_specs=[pl.BlockSpec(memory_space=VMEM)] * (leave_n * leave[1] + 1),
        out_shape=[jax.ShapeDtypeStruct((n // leave_n, part, channels), NARROW)] * (leave_n * leave[1])
        + [jax.ShapeDtypeStruct((total, channels), NARROW)],
        scratch_shapes=[VMEM((total, channels), NARROW)],
        compiler_params=params(10),
        cost_estimate=cost(2 * total * total * channels, 4 * total * channels),
        name=name,
    )(second_factor, *flat)
    return [out[p * leave_n : (p + 1) * leave_n] for p in range(leave[1])], out[-1]


def grads_kernel(mode, slots, group, half, held, w_ref, matrix_ref, *refs):
    n, length = w_ref.shape[1:]
    x_refs, refs = refs[:held], refs[held:]
    count = count_of(n, mode)
    slab_refs = refs[:count]
    refs = refs[count:] if half == 0 else refs[count + 2 :]
    vg_ref, fg_ref, slabs, back, fg_buf, out_buf, out_sem, fg_sem = refs
    part = slab_refs[0].shape[1]
    base = half * part
    steps = part // group
    rows = group * length

    def put(i, s):
        there = pl.ds(pl.multiple_of(base * length + i * rows, rows), rows)
        return pltpu.make_async_copy(out_buf.at[s], vg_ref.at[there, :], out_sem.at[s])

    every = n // count
    for o in range(count):
        for b in range(every):
            slabs[(o * every + b) * part : (o * every + b + 1) * part, :] = slab_refs[o][b]
    if matrix_ref.shape[0] == slabs.shape[0]:
        matrix = matrix_ref[...]
    else:
        matrix = merge_matrix(lax.axis_index("seq"), part, n, major(n, mode))
    back[...] = dot(matrix, slabs[...], ((1,), (0,))).astype(NARROW)

    each = steps // held

    def step(x_ref, start, early, i, carry):
        s = lax.rem(i, slots)

        @pl.when(i >= slots)
        def _():
            put(i - slots, s).wait()

        for g in range(group):
            block = i * group + g
            w = w_ref[base + block]
            f = back[pl.ds(pl.multiple_of(block * n, n), n), :]
            out_buf[s, g * length : (g + 1) * length, :] = dot(w, f, ((0,), (0,))).astype(NARROW)
            x = x_ref[pl.ds(pl.multiple_of((block - start * group) * length, length), length), :]
            fg_buf[block] = dot(f, x, ((1,), (1,))).astype(NARROW)
            if early and (g + 1) * 2 == group:
                piece(i, s, 0).start()
        if early:
            piece(i, s, 1).start()
        else:
            put(i, s).start()
        return carry

    def piece(i, s, p):
        size = rows // 2
        there = pl.ds(pl.multiple_of(base * length + i * rows + p * size, size), size)
        return pltpu.make_async_copy(out_buf.at[s, pl.ds(p * size, size), :], vg_ref.at[there, :], out_sem.at[s])

    for h in range(held):
        end = (h + 1) * each
        peeled = 1 if h == held - 1 and group % 2 == 0 else 0
        lax.fori_loop(h * each, end - peeled, functools.partial(step, x_refs[h], h * each, False), 0)
        if peeled:
            lax.fori_loop(end - 1, end, functools.partial(step, x_refs[h], h * each, True), 0)
    last = pltpu.make_async_copy(fg_buf, fg_ref.at[pl.ds(base, part)], fg_sem)
    last.start()
    for i in range(steps - slots, steps):
        put(i, i % slots).wait()
    last.wait()


def grads(first_factor, matrix, kept_x, slabs, mode, half, earlier):
    blocks, n, length = first_factor.shape
    channels = kept_x[0].shape[1]
    held, count = len(kept_x), len(slabs)
    part = slabs[0].shape[1]
    group = next(g for g in (4, 2, 1) if part % g == 0)
    slots = min(3, part // group)
    shapes = [
        jax.ShapeDtypeStruct((blocks * length, channels), NARROW),
        jax.ShapeDtypeStruct(first_factor.shape, NARROW),
    ]
    return pl.pallas_call(
        functools.partial(grads_kernel, mode, slots, group, half, held),
        in_specs=[pl.BlockSpec(memory_space=VMEM)] * (2 + held + count)
        + ([] if half == 0 else [pl.BlockSpec(memory_space=ANY)] * 2),
        out_specs=[pl.BlockSpec(memory_space=ANY)] * 2,
        out_shape=shapes,
        input_output_aliases={} if half == 0 else {2 + held + count: 0, 3 + held + count: 1},
        scratch_shapes=[
            VMEM((part * n, channels), NARROW),
            VMEM((part * n, channels), NARROW),
            VMEM((part, n, length), NARROW),
            VMEM((slots, group * length, channels), NARROW),
            pltpu.SemaphoreType.DMA((slots,)),
            pltpu.SemaphoreType.DMA,
        ],
        compiler_params=params(16),
        cost_estimate=cost(4 * part * n * length * channels, 2 * part * length * channels),
        name="grads",
    )(first_factor, matrix, *kept_x, *slabs, *(earlier or ()))


def gates_kernel(n, mode, pieces, matrix_ref, g_ref, d_ref, *refs):
    count = count_of(n, mode)
    slab_refs, (mixed_ref, grad_ref, slabs, mixed, grad, sem) = refs[:count], refs[count:]
    span = slab_refs[0].shape[0]
    for o in range(count):
        slabs[o * span : (o + 1) * span, :] = slab_refs[o][...]
    size = slabs.shape[0] // pieces
    copies = []
    for p in range(pieces):
        here = slice(p * size, (p + 1) * size)
        z = dot(matrix_ref[here, :], slabs[...], ((1,), (0,)))
        mixed[here, :] = (g_ref[here, :].astype(WIDE) * z).astype(NARROW)
        grad[here, :] = (d_ref[here, :].astype(WIDE) * z).astype(NARROW)
        copies.append(pltpu.make_async_copy(mixed.at[here, :], mixed_ref.at[here, :], sem.at[0, p]))
        copies.append(pltpu.make_async_copy(grad.at[here, :], grad_ref.at[here, :], sem.at[1, p]))
        copies[-2].start()
        copies[-1].start()
    for copy in copies:
        copy.wait()


def gates(matrix, gate_in, cotangent, slabs, mode):
    rows, n, channels = gate_in.shape
    total = rows * n
    count = count_of(n, mode)
    span = n // count * rows
    pieces = 2
    out = pl.pallas_call(
        functools.partial(gates_kernel, n, mode, pieces),
        in_specs=[pl.BlockSpec(memory_space=VMEM)] * (3 + count),
        out_specs=[pl.BlockSpec(memory_space=ANY)] * 2,
        out_shape=[jax.ShapeDtypeStruct((total, channels), NARROW)] * 2,
        scratch_shapes=[VMEM((total, channels), NARROW)] * 3 + [pltpu.SemaphoreType.DMA((2, pieces))],
        compiler_params=params(10),
        cost_estimate=cost(2 * total * total * channels, 10 * total * channels),
        name="gates",
    )(
        matrix,
        gate_in.reshape(total, channels),
        cotangent.reshape(total, channels),
        *[s.reshape(span, channels) for s in slabs],
    )
    return [o.reshape(gate_in.shape) for o in out]


def after(arrays, *tokens):
    return list(lax.optimization_barrier(tuple(arrays) + tokens)[: len(arrays)])


def regroup(slabs):
    count = slabs[0].shape[0]
    return [jnp.stack([s[b] for s in slabs]) for b in range(count)]


def by_permutes(values, gate_in, cotangent, first_factor, second_factor, inner):
    n = gate_in.shape[1]
    near, far = (True, inner), (False, inner)

    def permutes(slabs, step):
        got = list(slabs)
        for i in range(1, len(slabs)):
            got[i] = lax.ppermute(slabs[i], "seq", [(j, j ^ (ORDER[i] * step)) for j in range(n)])
        return got

    def across(slabs):
        return permutes(slabs, inner)

    def beside(slabs):
        return permutes(slabs, 1)

    gated = gated_slabs(gate_in, cotangent, far)
    e = across(gated)
    (factor,) = after([first_factor], gated[0])
    u, kept_x, merge_near, merge_far = inner_slabs(factor, values, far, (near, far))
    e = beside(regroup(after(e, u[0])))
    u = across(u)
    (f,), e_all = mix(second_factor, [e], n, (near, 1), (far, 1), True, "back")
    f = across(f)
    u = beside(regroup(u))
    (z,), u_all = mix(second_factor, [u], n, (near, 1), (near, 1), False, "forth")
    z = across(regroup(beside(z)))
    f = beside(regroup(f))
    values_grad, first_grad = grads(first_factor, merge_near, kept_x, f, near, 0, None)
    second_grad = dot(e_all, u_all, ((1,), (1,))).astype(NARROW)[None]
    gate_in, cotangent = after([gate_in, cotangent], first_grad)
    mixed, gate_grad = gates(merge_far, gate_in, cotangent, z, far)
    return mixed, values_grad, gate_grad, first_grad, second_grad


def by_all_to_all(values, gate_in, cotangent, first_factor, second_factor):
    block_len = first_factor.shape[2]
    channels = values.shape[1]
    blocks_x = values.reshape(-1, block_len, channels)
    inner = jnp.einsum("aqp,apc->aqc", first_factor, blocks_x, preferred_element_type=WIDE).astype(NARROW)
    gated = (gate_in.astype(WIDE) * cotangent.astype(WIDE)).astype(NARROW)
    inner_t = lax.all_to_all(inner, "seq", split_axis=1, concat_axis=0, tiled=True)
    outer_t = jnp.einsum("qxa,aqc->xqc", second_factor, inner_t, preferred_element_type=WIDE).astype(NARROW)
    outer = lax.all_to_all(outer_t, "seq", split_axis=0, concat_axis=1, tiled=True)
    gated_t = lax.all_to_all(gated, "seq", split_axis=1, concat_axis=0, tiled=True)
    second_grad = jnp.einsum("xqc,aqc->qxa", gated_t, inner_t, preferred_element_type=WIDE).astype(NARROW)
    back_t = jnp.einsum("qxa,xqc->aqc", second_factor, gated_t, preferred_element_type=WIDE).astype(NARROW)
    back_inner = lax.all_to_all(back_t, "seq", split_axis=0, concat_axis=1, tiled=True)
    outer_f = outer.astype(WIDE)
    mixed = (gate_in.astype(WIDE) * outer_f).astype(NARROW)
    gate_grad = (cotangent.astype(WIDE) * outer_f).astype(NARROW)
    first_grad = jnp.einsum("aqc,apc->aqp", back_inner, blocks_x, preferred_element_type=WIDE).astype(NARROW)
    values_grad = (
        jnp.einsum("aqp,aqc->apc", first_factor, back_inner, preferred_element_type=WIDE)
        .astype(NARROW)
        .reshape(-1, channels)
    )
    return mixed, values_grad, gate_grad, first_grad, second_grad


def solution(mesh):
    n = mesh.shape["seq"]

    def on_device(values, gate_in, cotangent, first_factor, second_factor):
        rows, kept = gate_in.shape[:2]
        if n == 16 and kept == n and rows % 32 == 0 and first_factor.shape[0] == rows:
            return by_permutes(values, gate_in, cotangent, first_factor, second_factor, 4)
        return by_all_to_all(values, gate_in, cotangent, first_factor, second_factor)

    both = ("grp", "seq")
    return jax.shard_map(
        on_device,
        mesh=mesh,
        in_specs=(
            P(both, None),
            P(both, None, None),
            P(both, None, None),
            P("seq", None, None),
            P("seq", None, None),
        ),
        out_specs=(
            P(both, None, None),
            P(both, None),
            P(both, None, None),
            P(both, None, None),
            P(both, None, None),
        ),
        check_vma=False,
    )
```
